512 devices in a mesh: loop: 32 (over y_hi, x, core), grp: 16 (over y_lo, z).
Axes of the slice: x: 4, y: 8 (y_hi: 4, y_lo: 2; y = y_hi * 2 + y_lo), z: 8, core: 2. Of those that a mesh axis runs over, the one named last changes fastest.
Arguments:
- image_emb: bfloat16 [8192, 1152], P(('loop', 'grp')), may hold values from -6 to 6
- text_emb: bfloat16 [8192, 1152], P(('loop', 'grp')), may hold values from -6 to 6
- log_scale: float32 [1], replicated, may hold values from 4.2 to 4.8
- bias: float32 [1], replicated, may hold values from -4 to -2
Outputs:
- image_grad: float32 [8192, 1152], P(('loop', 'grp'))
- text_grad: float32 [8192, 1152], P(('loop', 'grp'))
The draws below stay inside these ranges and needn't reach their ends.
All inputs are finite; a program needn't handle non-finite values.
Results may differ from the reference program's by a relative error of at most 0.008.
Values may be sent and summed in bfloat16 or wider, within the bound.
A program may use at most 64 MiB of HBM per device.

```python
import math
import jax
import jax.numpy as jnp
from jax import lax

D = 1152
BATCH = 8192


def shard_levels(rng, shape, shards, smallest, top_value):
    loudness = 1.0
    for position, parts in shards:
        draws = jax.random.uniform(jax.random.fold_in(jax.random.fold_in(rng, 6), position), (parts,), jnp.float32, smallest / len(shards), top_value / len(shards))
        loudness = loudness * jnp.repeat(jnp.exp(draws), shape[position] // parts).reshape((-1,) + (1,) * (len(shape) - 1 - position))
    return loudness


def gaussian(key, dims, width, bound, pieces=(), held_as=jnp.bfloat16):
    loudness = shard_levels(key, dims, pieces, -0.22, 0.18) if pieces else 1.0
    array = jax.random.normal(key, dims, jnp.float32) * width * loudness
    return jnp.minimum(jnp.maximum(array, -bound), bound).astype(held_as)


def setup_inputs(seed: int = 0) -> dict:
    arg_keys = jax.random.split(jax.random.key(seed), 5)
    return {
        "image_emb": gaussian(arg_keys[0], (BATCH, D), 1.0, 6.0, ((0, 512),)),
        "text_emb": gaussian(arg_keys[1], (BATCH, D), 1.0, 6.0, ((0, 512),)),
        "log_scale": jnp.clip(jax.random.uniform(arg_keys[2], (1,), jnp.float32, 4.2, 4.8), 4.2, 4.8),
        "bias": jnp.clip(jax.random.uniform(arg_keys[3], (1,), jnp.float32, -4.0, -2.0), -4.0, -2.0),
    }


EPS = 1e-06

def normalize(values):
    wide = values.astype(jnp.float32)
    length = jnp.sqrt(lax.optimization_barrier(jnp.sum(wide * wide, axis=-1, keepdims=True)) + EPS)
    return (wide / length, length)

def norm_back(unit_rows, length, upstream):
    along = lax.optimization_barrier(jnp.sum(unit_rows * upstream, axis=-1, keepdims=True))
    return (upstream - unit_rows * along) / length

def reference(image_emb, text_emb, log_scale, bias):
    img_unit, img_length = normalize(image_emb)
    txt_unit, txt_length = normalize(text_emb)
    img_low = img_unit.astype(jnp.bfloat16)
    txt_low = txt_unit.astype(jnp.bfloat16)
    logit_scale = jnp.exp(log_scale[0])
    offset = bias[0]
    total_rows = img_low.shape[0]
    block_size = math.gcd(total_rows, 512)
    block_count = total_rows // block_size
    column_ids = jnp.arange(total_rows, dtype=jnp.int32)

    def block_step(text_sum, row_start):
        row_block = lax.dynamic_slice_in_dim(img_low, row_start, block_size, 0)
        logits = logit_scale * jnp.dot(row_block, txt_low.T, preferred_element_type=jnp.float32) + offset
        row_ids = row_start + jnp.arange(block_size, dtype=jnp.int32)
        labels = (row_ids[:, None] == column_ids[None, :]).astype(jnp.float32)
        grad_low = (logit_scale * (jax.nn.sigmoid(logits) - labels)).astype(jnp.bfloat16)
        image_part = jnp.dot(grad_low, txt_low, preferred_element_type=jnp.float32)
        text_sum = text_sum + jnp.dot(grad_low.T, row_block, preferred_element_type=jnp.float32)
        return (text_sum, image_part)
    starts = (jnp.arange(block_count, dtype=jnp.int32) * block_size).astype(jnp.int32)
    text_sum, image_parts = lax.scan(block_step, jnp.zeros(txt_low.shape, jnp.float32), starts)
    image_sum = image_parts.reshape(img_low.shape)
    return (norm_back(img_unit, img_length, image_sum), norm_back(txt_unit, txt_length, text_sum))
```

```python
import jax
import jax.numpy as jnp
from jax import lax
from jax.experimental import pallas as pl
from jax.experimental.pallas import tpu as pltpu
from jax.sharding import PartitionSpec as P

EPS = 1e-06
ROWS = 16
RING = 8
OFFS = (4, 3, -3, 2, -2, 1, -1, 0)
OWN = 7
HALF = RING * ROWS
BF = jnp.bfloat16
F32 = jnp.float32


def slot_of(offset):
    return OFFS.index(4 if offset in (4, -4) else offset)


GZ, GY, GXI, GXT, GC = 0, 8, 16, 24, 32
RC, RXI, RXT, RZ, RY = 48, 52, 56, 60, 68
NSEM = 76
BATCH = 2
NBATCH = RING // BATCH


def kernel(
    img_hbm, txt_hbm, scale_ref, bias_ref, out_i, out_t,
    raw, unit, length, img, txt, grad, own_i, own_t,
    snd_c, snd_xi, snd_xt, snd_z, snd_y,
    rcv_c, rcv_xi, rcv_xt, rcv_z, rcv_y,
    in_sem, ssem, rsem,
):
    loop_at = lax.axis_index("loop")
    grp_at = lax.axis_index("grp")
    c = loop_at % 2
    x = (loop_at // 2) % 4
    y_hi = loop_at // 8
    y_lo = grp_at // 8
    z = grp_at % 8
    y = y_hi * 2 + y_lo

    def device(dx, dy, dz, dc):
        return {"loop": ((dy // 2) * 4 + dx) * 2 + dc, "grp": (dy % 2) * 8 + dz}

    z_peer = {o: device(x, y, (z + o + RING) % RING, c) for o in OFFS if o}
    y_peer = {o: device(x, (y + o + RING) % RING, z, c) for o in OFFS if o}
    xa_peer = device(x + 1 - 2 * (x % 2), y, z, c)
    xb_peer = device(3 - x, y, z, c)
    c_peer = device(x, y, z, 1 - c)

    barrier = pltpu.get_barrier_semaphore()
    peers = list(z_peer.values()) + list(y_peer.values()) + [xa_peer, xb_peer, c_peer]
    for peer in peers:
        pl.semaphore_signal(barrier, 1, device_id=peer, device_id_type=pl.DeviceIdType.MESH)

    loads = [
        pltpu.make_async_copy(img_hbm, raw.at[0], in_sem.at[0]),
        pltpu.make_async_copy(txt_hbm, raw.at[1], in_sem.at[1]),
    ]
    for load in loads:
        load.start()

    def rows(ref, quarter, slot, count=1):
        return ref.at[pl.ds(quarter * HALF + slot * ROWS, count * ROWS)]

    sent = []

    def send(src, dst, s_at, r_at, peer):
        copy = pltpu.make_async_remote_copy(
            src, dst, ssem.at[s_at], rsem.at[r_at],
            device_id=peer, device_id_type=pl.DeviceIdType.MESH,
        )
        copy.start()
        sent.append(copy)

    def wait_recv(dst, r_at):
        pltpu.make_async_remote_copy(
            dst, dst, ssem.at[0], rsem.at[r_at],
            device_id=c_peer, device_id_type=pl.DeviceIdType.MESH,
        ).wait_recv()

    for k, table in ((0, img), (1, txt)):
        loads[k].wait()
        wide = raw[k].astype(F32)
        norm = jnp.sqrt(jnp.sum(wide * wide, axis=-1, keepdims=True) + EPS)
        units = wide / norm
        unit[k] = units
        length[k] = norm
        table[pl.ds(OWN * ROWS, ROWS)] = units.astype(BF)

    pl.semaphore_wait(barrier, len(peers))

    for s, o in enumerate(OFFS[:-1]):
        t = slot_of(-o)
        send(rows(img, 0, OWN), rows(img, 0, t), GZ + s, GZ + t, z_peer[o])
        send(rows(txt, 0, OWN), rows(txt, 0, t), GY + s, GY + t, y_peer[o])
        if s == 0:
            send(rows(img, 0, OWN), rows(img, 1, OWN), GXI + OWN, GXI + OWN, xa_peer)
            send(rows(txt, 0, OWN), rows(txt, 1, OWN), GXT + OWN, GXT + OWN, xb_peer)
    send(rows(txt, 0, OWN), rows(txt, 2, OWN), GC + OWN, GC + OWN, c_peer)

    for s in reversed(range(OWN)):
        wait_recv(rows(txt, 0, s), GY + s)
        send(rows(txt, 0, s), rows(txt, 1, s), GXT + s, GXT + s, xb_peer)
        send(rows(txt, 0, s), rows(txt, 2, s), GC + s, GC + s, c_peer)
        wait_recv(rows(img, 0, s), GZ + s)
        send(rows(img, 0, s), rows(img, 1, s), GXI + s, GXI + s, xa_peer)
    for s in reversed(range(RING)):
        wait_recv(rows(txt, 1, s), GXT + s)
        send(rows(txt, 1, s), rows(txt, 3, s), GC + RING + s, GC + RING + s, c_peer)
    for s in reversed(range(RING)):
        wait_recv(rows(img, 1, s), GXI + s)
        wait_recv(rows(txt, 2, s), GC + s)
    for s in reversed(range(RING)):
        wait_recv(rows(txt, 3, s), GC + RING + s)

    scale = jnp.exp(jnp.full((1, 1), scale_ref[0], F32))
    offset = bias_ref[0]
    for q in range(4):
        dots = lax.dot_general(
            img[...], txt[pl.ds(q * HALF, HALF)], (((1,), (1,)), ((), ())), preferred_element_type=F32
        )
        prob = jax.nn.sigmoid(scale * dots + offset)
        if q == 0:
            i = lax.broadcasted_iota(jnp.int32, prob.shape, 0)
            j = lax.broadcasted_iota(jnp.int32, prob.shape, 1)
            prob = prob - jnp.where((i == j) & (i >= OWN * ROWS), 1.0, 0.0)
        grad[:, pl.ds(q * HALF, HALF)] = (scale * prob).astype(BF)

    def text_part(q):
        return lax.dot_general(
            grad[:, pl.ds(q * HALF, HALF)], img[...], (((0,), (0,)), ((), ())), preferred_element_type=F32
        )

    def image_part(q):
        return jnp.dot(grad[pl.ds(q * HALF, HALF), :], txt[...], preferred_element_type=F32)

    for h in (1, 0):
        snd_c[pl.ds(h * HALF, HALF)] = text_part(2 + h).astype(BF)
        send(rows(snd_c, h, 0, RING), rows(rcv_c, h, 0, RING), RC + h, RC + h, c_peer)
    snd_xi[...] = image_part(1).astype(BF)
    for b in range(NBATCH):
        part = pl.ds(b * BATCH * ROWS, BATCH * ROWS)
        send(snd_xi.at[part], rcv_xi.at[part], RXI + b, RXI + b, xa_peer)
    own_t[...] = text_part(1)
    wait_recv(rows(rcv_c, 1, 0, RING), RC + 1)
    for b in range(NBATCH):
        part = pl.ds(b * BATCH * ROWS, BATCH * ROWS)
        snd_xt[part] = (own_t[part] + rcv_c[pl.ds(HALF + b * BATCH * ROWS, BATCH * ROWS)].astype(F32)).astype(BF)
        send(snd_xt.at[part], rcv_xt.at[part], RXT + b, RXT + b, xb_peer)
    own_i[...] = image_part(0)
    own_t[...] = text_part(0)
    wait_recv(rows(rcv_c, 0, 0, RING), RC + 0)
    own_t[...] += rcv_c[pl.ds(0, HALF)].astype(F32)
    for b in range(NBATCH):
        part = pl.ds(b * BATCH * ROWS, BATCH * ROWS)
        for own, snd, rcv_x, rcv, sem_x, sem, peer in (
            (own_i, snd_z, rcv_xi, rcv_z, RXI, RZ, z_peer),
            (own_t, snd_y, rcv_xt, rcv_y, RXT, RY, y_peer),
        ):
            wait_recv(rcv_x.at[part], sem_x + b)
            own[part] += rcv_x[part].astype(F32)
            snd[part] = own[part].astype(BF)
            for s in range(b * BATCH, (b + 1) * BATCH):
                if s != OWN:
                    t = slot_of(-OFFS[s])
                    send(rows(snd, 0, s), rows(rcv, 0, t), sem + s, sem + t, peer[OFFS[s]])

    for k, (own, rcv, sem, out) in enumerate(((own_i, rcv_z, RZ, out_i), (own_t, rcv_y, RY, out_t))):
        total = own[pl.ds(OWN * ROWS, ROWS)]
        for s in range(OWN):
            wait_recv(rows(rcv, 0, s), sem + s)
            total = total + rcv[pl.ds(s * ROWS, ROWS)].astype(F32)
        units = unit[k]
        along = jnp.sum(units * total, axis=-1, keepdims=True)
        out[...] = (total - units * along) / length[k]
    for copy in sent:
        copy.wait_send()


def per_device(image_emb, text_emb, log_scale, bias):
    rows, width = image_emb.shape
    out = jax.ShapeDtypeStruct((rows, width), F32)
    vmem = lambda n, dtype: pltpu.VMEM((n, width), dtype)
    return pl.pallas_call(
        kernel,
        out_shape=(out, out),
        in_specs=[pl.BlockSpec(memory_space=pl.ANY)] * 2 + [pl.BlockSpec(memory_space=pltpu.SMEM)] * 2,
        out_specs=(pl.BlockSpec(memory_space=pltpu.VMEM),) * 2,
        scratch_shapes=[
            pltpu.VMEM((2, rows, width), BF),
            pltpu.VMEM((2, rows, width), F32),
            pltpu.VMEM((2, rows, 1), F32),
            vmem(2 * HALF, BF),
            vmem(4 * HALF, BF),
            pltpu.VMEM((2 * HALF, 4 * HALF), BF),
            vmem(HALF, F32),
            vmem(HALF, F32),
            vmem(2 * HALF, BF),
            vmem(HALF, BF),
            vmem(HALF, BF),
            vmem(HALF, BF),
            vmem(HALF, BF),
            vmem(2 * HALF, BF),
            vmem(HALF, BF),
            vmem(HALF, BF),
            vmem(HALF, BF),
            vmem(HALF, BF),
            pltpu.SemaphoreType.DMA((2,)),
            pltpu.SemaphoreType.DMA((NSEM,)),
            pltpu.SemaphoreType.DMA((NSEM,)),
        ],
        compiler_params=pltpu.CompilerParams(
            collective_id=0, has_side_effects=True, vmem_limit_bytes=48 * 2**20
        ),
        name="siglip_grads",
    )(image_emb, text_emb, log_scale, bias)


def solution(mesh):
    return jax.shard_map(
        per_device,
        mesh=mesh,
        in_specs=(P(("loop", "grp"), None), P(("loop", "grp"), None), P(), P()),
        out_specs=(P(("loop", "grp"), None), P(("loop", "grp"), None)),
        check_vma=False,
    )
```

```python
import jax
import jax.numpy as jnp
from jax import lax
from jax.experimental import pallas as pl
from jax.experimental.pallas import tpu as pltpu
from jax.sharding import PartitionSpec as P

EPS = 1e-06
ROWS = 16
RING = 8
OFFS = (4, 3, -3, 2, -2, 1, -1, 0)
OWN = 7
HALF = RING * ROWS
BF = jnp.bfloat16
F32 = jnp.float32


def slot_of(offset):
    return OFFS.index(4 if offset in (4, -4) else offset)


XPARTS = ((1, 3), (3, 8))
GI, GT, GXI, GXT, GC = 0, 8, 16, 24, 32
RC, RXI, RXT, RI, RT, RFI, RFT = 48, 52, 60, 68, 76, 84, 86
NRECV = 88
NSEND = 100


def kernel(
    img_hbm, txt_hbm, scale_ref, bias_ref, out_i, out_t,
    raw, unit, length, img, txt, grad, own_i, own_t,
    snd_c, snd_xi, snd_xt, snd_ri, snd_rt,
    rcv_c, rcv_xi, rcv_xt, rcv_ri, rcv_rt, rcv_fi, rcv_ft,
    in_sem, ssem, rsem,
):
    loop_at = lax.axis_index("loop")
    grp_at = lax.axis_index("grp")
    c = loop_at % 2
    x = (loop_at // 2) % 4
    y_hi = loop_at // 8
    y_lo = grp_at // 8
    z = grp_at % 8
    y = y_hi * 2 + y_lo

    def device(dx, dy, dz, dc):
        return {"loop": ((dy // 2) * 4 + dx) * 2 + dc, "grp": (dy % 2) * 8 + dz}

    i_peer = {o: device(x, (y + o + RING) % RING, z, c) for o in OFFS[1:-1]}
    t_peer = {o: device(x, y, (z + o + RING) % RING, c) for o in OFFS[1:-1]}
    xa = x + 1 - 2 * (x % 2)
    xb = 3 - x
    xa_peer = device(xa, y, z, c)
    xb_peer = device(xb, y, z, c)
    xi_peer = device(xa, (y - 1 + RING) % RING, z, c)
    xt_peer = device(xb, y, (z - 1 + RING) % RING, c)
    xi_from = device(xa, (y + 1) % RING, z, c)
    xt_from = device(xb, y, (z + 1) % RING, c)
    c_peer = device(x, y, z, 1 - c)

    loads = [
        pltpu.make_async_copy(img_hbm, raw.at[0], in_sem.at[0]),
        pltpu.make_async_copy(txt_hbm, raw.at[1], in_sem.at[1]),
    ]
    for load in loads:
        load.start()

    barrier = pltpu.get_barrier_semaphore()
    peers = list(i_peer.values()) + list(t_peer.values()) + [xa_peer, xb_peer, c_peer, xi_peer, xi_from, xt_peer, xt_from]
    for peer in peers:
        pl.semaphore_signal(barrier, 1, device_id=peer, device_id_type=pl.DeviceIdType.MESH)

    def rows(ref, quarter, slot, count=1):
        return ref.at[pl.ds(quarter * HALF + slot * ROWS, count * ROWS)]

    sent = []

    def send(src, dst, r_at, peer):
        copy = pltpu.make_async_remote_copy(
            src, dst, ssem.at[len(sent)], rsem.at[r_at],
            device_id=peer, device_id_type=pl.DeviceIdType.MESH,
        )
        copy.start()
        sent.append(copy)

    def wait_recv(dst, r_at):
        pltpu.make_async_remote_copy(
            dst, dst, ssem.at[0], rsem.at[r_at],
            device_id=c_peer, device_id_type=pl.DeviceIdType.MESH,
        ).wait_recv()

    def normalize(k, table):
        loads[k].wait()
        wide = raw[k].astype(F32)
        norm = jnp.sqrt(jnp.sum(wide * wide, axis=-1, keepdims=True) + EPS)
        units = wide / norm
        unit[k] = units
        length[k] = norm
        table[pl.ds(OWN * ROWS, ROWS)] = units.astype(BF)

    normalize(1, txt)
    normalize(0, img)
    pl.semaphore_wait(barrier, len(peers))
    def text_part(q):
        return lax.dot_general(
            grad[:, pl.ds(q * HALF, HALF)], img[...], (((0,), (0,)), ((), ())), preferred_element_type=F32
        )

    def image_part(q):
        return jnp.dot(grad[pl.ds(q * HALF, HALF), :], txt[...], preferred_element_type=F32)

    def gather():
        send(rows(txt, 0, OWN), rows(txt, 1, OWN), GXT + OWN, xb_peer)
        send(rows(img, 0, OWN), rows(img, 1, OWN), GXI + OWN, xa_peer)
        send(rows(txt, 0, OWN), rows(txt, 2, OWN), GC + OWN, c_peer)
        for s in range(1, OWN):
            o = OFFS[s]
            t = slot_of(-o)
            send(rows(txt, 0, OWN), rows(txt, 0, t), GT + t, t_peer[o])
            send(rows(img, 0, OWN), rows(img, 0, t), GI + t, i_peer[o])
        wait_recv(rows(txt, 0, 1), GT + 1)
        send(rows(txt, 0, 1), rows(txt, 0, 0), GT, t_peer[-1])
        wait_recv(rows(img, 0, 1), GI + 1)
        send(rows(img, 0, 1), rows(img, 0, 0), GI, i_peer[-1])
        parts = ((1, 3), (3, OWN), (0, 1))
        for lo, hi in parts:
            n = hi - lo
            for s in range(lo, hi):
                if s != 1:
                    wait_recv(rows(txt, 0, s), GT + s)
            send(rows(txt, 0, lo, n), rows(txt, 1, lo, n), GXT + lo, xb_peer)
            send(rows(txt, 0, lo, n), rows(txt, 2, lo, n), GC + lo, c_peer)
            for s in range(lo, hi):
                if s != 1:
                    wait_recv(rows(img, 0, s), GI + s)
            send(rows(img, 0, lo, n), rows(img, 1, lo, n), GXI + lo, xa_peer)
        parts = ((OWN, RING), *parts)
        for lo, hi in parts:
            n = hi - lo
            wait_recv(rows(txt, 1, lo, n), GXT + lo)
            send(rows(txt, 1, lo, n), rows(txt, 3, lo, n), GC + RING + lo, c_peer)
        for lo, hi in parts:
            n = hi - lo
            wait_recv(rows(img, 1, lo, n), GXI + lo)
            wait_recv(rows(txt, 2, lo, n), GC + lo)
            wait_recv(rows(txt, 3, lo, n), GC + RING + lo)

    def grads():
        scale = jnp.exp(jnp.full((1, 1), scale_ref[0], F32))
        offset = bias_ref[0]
        for q in range(4):
            dots = lax.dot_general(
                img[...], txt[pl.ds(q * HALF, HALF)], (((1,), (1,)), ((), ())), preferred_element_type=F32
            )
            prob = jax.nn.sigmoid(scale * dots + offset)
            if q == 0:
                i = lax.broadcasted_iota(jnp.int32, prob.shape, 0)
                j = lax.broadcasted_iota(jnp.int32, prob.shape, 1)
                prob = prob - jnp.where((i == j) & (i >= OWN * ROWS), 1.0, 0.0)
            grad[:, pl.ds(q * HALF, HALF)] = (scale * prob).astype(BF)

    def reduce():
        def span(lo, hi):
            return pl.ds(lo * ROWS, (hi - lo) * ROWS)

        def cross(snd, rcv_x, rcv_f, sem_x, sem_f, peer, far_peer):
            send(rows(snd, 0, 0), rows(rcv_f, 0, 1), sem_f + 1, far_peer)
            for lo, hi in XPARTS:
                send(rows(snd, 0, lo, hi - lo), rows(rcv_x, 0, lo, hi - lo), sem_x + lo, peer)

        def far(own, snd, rcv_f, sem_f, peer):
            snd[span(0, 1)] = own[span(0, 1)].astype(BF)
            send(rows(snd, 0, 0), rows(rcv_f, 0, 0), sem_f, peer[1])

        def spread(own, snd, rcv_x, rcv_f, rcv, sem_x, sem_f, sem, peer, lo, hi):
            at = span(lo, hi)
            wait_recv(rcv_x.at[at], sem_x + lo)
            own[at] += rcv_x[at].astype(F32)
            if lo == 1:
                wait_recv(rows(rcv_f, 0, 0), sem_f)
                wait_recv(rows(rcv_f, 0, 1), sem_f + 1)
                own[span(1, 3)] += rcv_f[...].astype(F32)
            snd[at] = own[at].astype(BF)
            for s in range(lo, min(hi, OWN)):
                t = slot_of(-OFFS[s])
                send(rows(snd, 0, s), rows(rcv, 0, t), sem + t, peer[OFFS[s]])

        for h in (1, 0):
            snd_c[pl.ds(h * HALF, HALF)] = text_part(2 + h).astype(BF)
            send(rows(snd_c, h, 0, RING), rows(rcv_c, h, 0, RING), RC + h, c_peer)
        snd_xi[...] = image_part(1).astype(BF)
        cross(snd_xi, rcv_xi, rcv_fi, RXI, RFI, xa_peer, xi_peer)
        own_i[...] = image_part(0)
        far(own_i, snd_ri, rcv_fi, RFI, i_peer)
        own_t[...] = text_part(1)
        wait_recv(rows(rcv_c, 1, 0, RING), RC + 1)
        snd_xt[...] = (own_t[...] + rcv_c[pl.ds(HALF, HALF)].astype(F32)).astype(BF)
        cross(snd_xt, rcv_xt, rcv_ft, RXT, RFT, xb_peer, xt_peer)
        own_t[...] = text_part(0)
        wait_recv(rows(rcv_c, 0, 0, RING), RC + 0)
        own_t[...] += rcv_c[pl.ds(0, HALF)].astype(F32)
        far(own_t, snd_rt, rcv_ft, RFT, t_peer)
        for lo, hi in XPARTS:
            spread(own_i, snd_ri, rcv_xi, rcv_fi, rcv_ri, RXI, RFI, RI, i_peer, lo, hi)
            spread(own_t, snd_rt, rcv_xt, rcv_ft, rcv_rt, RXT, RFT, RT, t_peer, lo, hi)

    def finish():
        for k, (own, rcv, sem, out) in enumerate(((own_i, rcv_ri, RI, out_i), (own_t, rcv_rt, RT, out_t))):
            total = own[pl.ds(OWN * ROWS, ROWS)]
            for s in range(1, OWN):
                wait_recv(rows(rcv, 0, s), sem + s)
                total = total + rcv[pl.ds(s * ROWS, ROWS)].astype(F32)
            units = unit[k]
            along = jnp.sum(units * total, axis=-1, keepdims=True)
            out[...] = (total - units * along) / length[k]
    def drain():
        for copy in sent:
            copy.wait_send()
        sent.clear()

    gather()
    grads()
    reduce()
    finish()
    drain()


def per_device(image_emb, text_emb, log_scale, bias):
    rows, width = image_emb.shape
    out = jax.ShapeDtypeStruct((rows, width), F32)
    vmem = lambda n, dtype: pltpu.VMEM((n, width), dtype)
    return pl.pallas_call(
        kernel,
        out_shape=(out, out),
        in_specs=[pl.BlockSpec(memory_space=pl.ANY)] * 2 + [pl.BlockSpec(memory_space=pltpu.SMEM)] * 2,
        out_specs=(pl.BlockSpec(memory_space=pltpu.VMEM),) * 2,
        scratch_shapes=[
            pltpu.VMEM((2, rows, width), BF),
            pltpu.VMEM((2, rows, width), F32),
            pltpu.VMEM((2, rows, 1), F32),
            vmem(2 * HALF, BF),
            vmem(4 * HALF, BF),
            pltpu.VMEM((2 * HALF, 4 * HALF), BF),
            vmem(HALF, F32),
            vmem(HALF, F32),
            vmem(2 * HALF, BF),
            vmem(HALF, BF),
            vmem(HALF, BF),
            vmem(HALF, BF),
            vmem(HALF, BF),
            vmem(2 * HALF, BF),
            vmem(HALF, BF),
            vmem(HALF, BF),
            vmem(HALF, BF),
            vmem(HALF, BF),
            vmem(2 * ROWS, BF),
            vmem(2 * ROWS, BF),
            pltpu.SemaphoreType.DMA((2,)),
            pltpu.SemaphoreType.DMA((NSEND,)),
            pltpu.SemaphoreType.DMA((NRECV,)),
        ],
        compiler_params=pltpu.CompilerParams(
            collective_id=0, has_side_effects=True, vmem_limit_bytes=48 * 2**20
        ),
        name="siglip_grads",
    )(
        pltpu.with_memory_space_constraint(image_emb, pltpu.HBM),
        pltpu.with_memory_space_constraint(text_emb, pltpu.HBM),
        log_scale,
        bias,
    )


def solution(mesh):
    return jax.shard_map(
        per_device,
        mesh=mesh,
        in_specs=(P(("loop", "grp"), None), P(("loop", "grp"), None), P(), P()),
        out_specs=(P(("loop", "grp"), None), P(("loop", "grp"), None)),
        check_vma=False,
    )
```

```python
import jax
import jax.numpy as jnp
from jax import lax
from jax.experimental import pallas as pl
from jax.experimental.pallas import tpu as pltpu
from jax.sharding import PartitionSpec as P

EPS = 1e-06
ROWS = 16
RING = 8
OFFS = (4, 3, -3, 2, -2, 1, -1, 0)
OWN = 7
HALF = RING * ROWS
BF = jnp.bfloat16
F32 = jnp.float32


def slot_of(offset):
    return OFFS.index(4 if offset in (4, -4) else offset)


NEAR = (5, 6, 3, 4)
GI, GT, GXI, GXT, GC = 0, 8, 16, 24, 32
RC, RXI, RXT, RI, RT, RFI, RFT, RDI, RDT = 48, 52, 53, 54, 62, 70, 72, 74, 82
NRECV = 90
NSEND = 100


def kernel(
    img_hbm, txt_hbm, scale_ref, bias_ref, out_i, out_t,
    raw, unit, length, img, txt, grad, own_i, own_t,
    snd_c, snd_xi, snd_xt, snd_ri, snd_rt, snd_li, snd_lt,
    rcv_c, rcv_xi, rcv_xt, rcv_ri, rcv_rt, rcv_fi, rcv_ft, rcv_di, rcv_dt,
    in_sem, ssem, rsem,
):
    loop_at = lax.axis_index("loop")
    grp_at = lax.axis_index("grp")
    c = loop_at % 2
    x = (loop_at // 2) % 4
    y_hi = loop_at // 8
    y_lo = grp_at // 8
    z = grp_at % 8
    y = y_hi * 2 + y_lo

    def device(dx, dy, dz, dc):
        return {"loop": ((dy // 2) * 4 + dx) * 2 + dc, "grp": (dy % 2) * 8 + dz}

    i_peer = {o: device(x, (y + o + RING) % RING, z, c) for o in OFFS[1:-1]}
    t_peer = {o: device(x, y, (z + o + RING) % RING, c) for o in OFFS[1:-1]}
    xa = x + 1 - 2 * (x % 2)
    xb = 3 - x
    xa_peer = device(xa, y, z, c)
    xb_peer = device(xb, y, z, c)
    xi_peer = {o: device(xa, (y + o + RING) % RING, z, c) for o in (1, -1, 2, -2)}
    xt_peer = {o: device(xb, y, (z + o + RING) % RING, c) for o in (1, -1, 2, -2)}
    c_peer = device(x, y, z, 1 - c)

    loads = [
        pltpu.make_async_copy(img_hbm, raw.at[0], in_sem.at[0]),
        pltpu.make_async_copy(txt_hbm, raw.at[1], in_sem.at[1]),
    ]
    for load in loads:
        load.start()

    barrier = pltpu.get_barrier_semaphore()
    peers = []
    for o in (3, -3, 2, -2, 1, -1):
        peers += [table[o] for table in (t_peer, i_peer, xt_peer, xi_peer) if o in table]
    peers += [xb_peer, xa_peer, c_peer]
    for peer in peers:
        pl.semaphore_signal(barrier, 1, device_id=peer, device_id_type=pl.DeviceIdType.MESH)

    def rows(ref, quarter, slot, count=1):
        return ref.at[pl.ds(quarter * HALF + slot * ROWS, count * ROWS)]

    sent = []

    def send(src, dst, r_at, peer):
        copy = pltpu.make_async_remote_copy(
            src, dst, ssem.at[len(sent)], rsem.at[r_at],
            device_id=peer, device_id_type=pl.DeviceIdType.MESH,
        )
        copy.start()
        sent.append(copy)

    def wait_recv(dst, r_at):
        pltpu.make_async_remote_copy(
            dst, dst, ssem.at[0], rsem.at[r_at],
            device_id=c_peer, device_id_type=pl.DeviceIdType.MESH,
        ).wait_recv()

    def normalize(k, table):
        loads[k].wait()
        wide = raw[k].astype(F32)
        norm = jnp.sqrt(jnp.sum(wide * wide, axis=-1, keepdims=True) + EPS)
        units = wide / norm
        unit[k] = units
        length[k] = norm
        table[pl.ds(OWN * ROWS, ROWS)] = units.astype(BF)

    normalize(1, txt)
    pl.semaphore_wait(barrier, len(peers))
    def span(lo, hi):
        return pl.ds(lo * ROWS, (hi - lo) * ROWS)

    def text_part(q, lo, hi):
        part = grad[:, pl.ds(q * HALF + lo * ROWS, (hi - lo) * ROWS)]
        return lax.dot_general(part, img[...], (((0,), (0,)), ((), ())), preferred_element_type=F32)

    def image_part(q, lo, hi):
        part = grad[pl.ds(q * HALF + lo * ROWS, (hi - lo) * ROWS), :]
        return jnp.dot(part, txt[...], preferred_element_type=F32)

    def gather():
        sides = (
            (txt, GT, GXT, t_peer, xt_peer, xb_peer),
            (img, GI, GXI, i_peer, xi_peer, xa_peer),
        )
        for ref, sem, sem_x, ring, diag, pair in sides:
            if ref is img:
                normalize(0, img)
            for s in (1, 2):
                t = slot_of(-OFFS[s])
                send(rows(ref, 0, OWN), rows(ref, 0, t), sem + t, ring[OFFS[s]])
        for ref, sem, sem_x, ring, diag, pair in sides:
            send(rows(ref, 0, OWN), rows(ref, 1, OWN), sem_x + OWN, pair)
        for s in NEAR:
            for ref, sem, sem_x, ring, diag, pair in sides:
                t = slot_of(-OFFS[s])
                send(rows(ref, 0, OWN), rows(ref, 0, t), sem + t, ring[OFFS[s]])
                send(rows(ref, 0, OWN), rows(ref, 1, t), sem_x + t, diag[OFFS[s]])
        for ref, sem, sem_x, ring, diag, pair in sides:
            wait_recv(rows(ref, 0, 1), sem + 1)
            send(rows(ref, 0, 1), rows(ref, 0, 0), sem, ring[-1])
            send(rows(ref, 0, 1), rows(ref, 1, 0), sem_x, diag[-1])
            wait_recv(rows(ref, 0, 2), sem + 2)
            send(rows(ref, 0, 1, 2), rows(ref, 1, 1, 2), sem_x + 1, pair)

        def share(q, lo, n):
            send(rows(txt, q, lo, n), rows(txt, 2 + q, lo, n), GC + q * RING + lo, c_peer)

        share(0, 1, 2)
        for q, sem in ((0, GT), (1, GXT)):
            for s in NEAR:
                wait_recv(rows(txt, q, s), sem + s)
            if q == 1:
                wait_recv(rows(txt, q, OWN), sem + OWN)
            share(q, 3, 5)
        wait_recv(rows(txt, 0, 0), GT)
        share(0, 0, 1)
        wait_recv(rows(txt, 1, 1, 2), GXT + 1)
        share(1, 1, 2)
        wait_recv(rows(txt, 1, 0), GXT)
        share(1, 0, 1)
        for q, sem in ((0, GI), (1, GXI)):
            for s in NEAR:
                wait_recv(rows(img, q, s), sem + s)
            wait_recv(rows(img, q, 0), sem)
        wait_recv(rows(img, 1, OWN), GXI + OWN)
        wait_recv(rows(img, 1, 1, 2), GXI + 1)

    def gather_end():
        for q in (0, 1):
            for lo, n in ((3, 5), (1, 2), (0, 1)):
                wait_recv(rows(txt, 2 + q, lo, n), GC + q * RING + lo)

    def grads():
        scale = jnp.exp(jnp.full((1, 1), scale_ref[0], F32))
        offset = bias_ref[0]
        for q in range(4):
            if q == 2:
                gather_end()
            dots = lax.dot_general(
                img[...], txt[pl.ds(q * HALF, HALF)], (((1,), (1,)), ((), ())), preferred_element_type=F32
            )
            prob = jax.nn.sigmoid(scale * dots + offset)
            if q == 0:
                i = lax.broadcasted_iota(jnp.int32, prob.shape, 0)
                j = lax.broadcasted_iota(jnp.int32, prob.shape, 1)
                prob = prob - jnp.where((i == j) & (i >= OWN * ROWS), 1.0, 0.0)
            grad[:, pl.ds(q * HALF, HALF)] = (scale * prob).astype(BF)

    def reduce():
        def cross_far(snd, rcv_x, rcv_f, sem_x, sem_f, pair, diag):
            send(rows(snd, 0, 1, 2), rcv_x, sem_x, pair)
            send(rows(snd, 0, 0), rows(rcv_f, 0, 1), sem_f + 1, diag[-1])

        def along_far(snd, rcv_f, sem_f, ring):
            send(rows(snd, 0, 0), rows(rcv_f, 0, 0), sem_f, ring[1])

        def near(snd_x, snd, rcv_d, rcv, sem_d, sem, pair, diag, ring):
            for s in NEAR:
                t = slot_of(-OFFS[s])
                send(rows(snd_x, 0, s), rows(rcv_d, 0, t), sem_d + t, diag[OFFS[s]])
                send(rows(snd, 0, s), rows(rcv, 0, t), sem + t, ring[OFFS[s]])
            send(rows(snd_x, 0, OWN), rows(rcv_d, 0, OWN), sem_d + OWN, pair)

        def last(own, snd_l, rcv_x, rcv_f, rcv, sem_x, sem_f, sem, ring):
            wait_recv(rcv_x, sem_x)
            wait_recv(rows(rcv_f, 0, 0), sem_f)
            wait_recv(rows(rcv_f, 0, 1), sem_f + 1)
            snd_l[...] = (own[span(1, 3)] + rcv_x[...].astype(F32) + rcv_f[...].astype(F32)).astype(BF)
            for s in (1, 2):
                t = slot_of(-OFFS[s])
                send(rows(snd_l, 0, s - 1), rows(rcv, 0, t), sem + t, ring[OFFS[s]])

        def core_out(lo, hi, sem):
            for h in (1, 0):
                at = pl.ds(h * HALF + lo * ROWS, (hi - lo) * ROWS)
                snd_c[at] = text_part(2 + h, lo, hi).astype(BF)
                send(snd_c.at[at], rcv_c.at[at], sem + h, c_peer)

        def core_in(h, lo, hi, sem):
            at = pl.ds(h * HALF + lo * ROWS, (hi - lo) * ROWS)
            wait_recv(rcv_c.at[at], sem + h)
            return rcv_c[at].astype(F32)

        far, rest = (0, 3), (3, RING)
        core_out(*far, RC)
        snd_xi[span(*far)] = image_part(1, *far).astype(BF)
        cross_far(snd_xi, rcv_xi, rcv_fi, RXI, RFI, xa_peer, xi_peer)
        own_i[span(*far)] = image_part(0, *far)
        snd_ri[span(0, 1)] = own_i[span(0, 1)].astype(BF)
        along_far(snd_ri, rcv_fi, RFI, i_peer)
        cross_t = text_part(1, *far)
        along_t = text_part(0, *far)
        snd_xt[span(*far)] = (cross_t + core_in(1, *far, RC)).astype(BF)
        cross_far(snd_xt, rcv_xt, rcv_ft, RXT, RFT, xb_peer, xt_peer)
        own_t[span(*far)] = along_t + core_in(0, *far, RC)
        snd_rt[span(0, 1)] = own_t[span(0, 1)].astype(BF)
        along_far(snd_rt, rcv_ft, RFT, t_peer)
        core_out(*rest, RC + 2)
        snd_xi[span(*rest)] = image_part(1, *rest).astype(BF)
        own_i[span(*rest)] = image_part(0, *rest)
        snd_ri[span(*rest)] = own_i[span(*rest)].astype(BF)
        near(snd_xi, snd_ri, rcv_di, rcv_ri, RDI, RI, xa_peer, xi_peer, i_peer)
        snd_xt[span(*rest)] = (text_part(1, *rest) + core_in(1, *rest, RC + 2)).astype(BF)
        own_t[span(*rest)] = text_part(0, *rest) + core_in(0, *rest, RC + 2)
        snd_rt[span(*rest)] = own_t[span(*rest)].astype(BF)
        near(snd_xt, snd_rt, rcv_dt, rcv_rt, RDT, RT, xb_peer, xt_peer, t_peer)
        last(own_i, snd_li, rcv_xi, rcv_fi, rcv_ri, RXI, RFI, RI, i_peer)
        last(own_t, snd_lt, rcv_xt, rcv_ft, rcv_rt, RXT, RFT, RT, t_peer)

    def finish():
        tables = (
            (own_i, rcv_ri, rcv_di, RI, RDI, out_i),
            (own_t, rcv_rt, rcv_dt, RT, RDT, out_t),
        )
        totals = []
        for own, rcv, rcv_d, sem, sem_d, out in tables:
            total = own[pl.ds(OWN * ROWS, ROWS)]
            for s in (OWN, *NEAR):
                wait_recv(rows(rcv_d, 0, s), sem_d + s)
                total = total + rcv_d[pl.ds(s * ROWS, ROWS)].astype(F32)
                if s != OWN:
                    wait_recv(rows(rcv, 0, s), sem + s)
                    total = total + rcv[pl.ds(s * ROWS, ROWS)].astype(F32)
            totals.append(total)
        for k, (own, rcv, rcv_d, sem, sem_d, out) in enumerate(tables):
            total = totals[k]
            for s in (1, 2):
                wait_recv(rows(rcv, 0, s), sem + s)
                total = total + rcv[pl.ds(s * ROWS, ROWS)].astype(F32)
            units = unit[k]
            along = jnp.sum(units * total, axis=-1, keepdims=True)
            out[...] = (total - units * along) / length[k]

    def drain():
        for copy in sent:
            copy.wait_send()
        sent.clear()

    gather()
    grads()
    reduce()
    finish()
    drain()


def per_device(image_emb, text_emb, log_scale, bias):
    rows, width = image_emb.shape
    out = jax.ShapeDtypeStruct((rows, width), F32)
    vmem = lambda n, dtype: pltpu.VMEM((n, width), dtype)
    return pl.pallas_call(
        kernel,
        out_shape=(out, out),
        in_specs=[pl.BlockSpec(memory_space=pl.ANY)] * 2 + [pl.BlockSpec(memory_space=pltpu.SMEM)] * 2,
        out_specs=(pl.BlockSpec(memory_space=pltpu.VMEM),) * 2,
        scratch_shapes=[
            pltpu.VMEM((2, rows, width), BF),
            pltpu.VMEM((2, rows, width), F32),
            pltpu.VMEM((2, rows, 1), F32),
            vmem(2 * HALF, BF),
            vmem(4 * HALF, BF),
            pltpu.VMEM((2 * HALF, 4 * HALF), BF),
            vmem(HALF, F32),
            vmem(HALF, F32),
            vmem(2 * HALF, BF),
            vmem(HALF, BF),
            vmem(HALF, BF),
            vmem(HALF, BF),
            vmem(HALF, BF),
            vmem(2 * ROWS, BF),
            vmem(2 * ROWS, BF),
            vmem(2 * HALF, BF),
            vmem(2 * ROWS, BF),
            vmem(2 * ROWS, BF),
            vmem(HALF, BF),
            vmem(HALF, BF),
            vmem(2 * ROWS, BF),
            vmem(2 * ROWS, BF),
            vmem(HALF, BF),
            vmem(HALF, BF),
            pltpu.SemaphoreType.DMA((2,)),
            pltpu.SemaphoreType.DMA((NSEND,)),
            pltpu.SemaphoreType.DMA((NRECV,)),
        ],
        compiler_params=pltpu.CompilerParams(
            collective_id=0, has_side_effects=True, vmem_limit_bytes=48 * 2**20
        ),
        name="siglip_grads",
    )(
        pltpu.with_memory_space_constraint(image_emb, pltpu.HBM),
        pltpu.with_memory_space_constraint(text_emb, pltpu.HBM),
        log_scale,
        bias,
    )


def solution(mesh):
    return jax.shard_map(
        per_device,
        mesh=mesh,
        in_specs=(P(("loop", "grp"), None), P(("loop", "grp"), None), P(), P()),
        out_specs=(P(("loop", "grp"), None), P(("loop", "grp"), None)),
        check_vma=False,
    )
```

```python
import jax
import jax.numpy as jnp
from jax import lax
from jax.experimental import pallas as pl
from jax.experimental.pallas import tpu as pltpu
from jax.sharding import PartitionSpec as P

EPS = 1e-06
ROWS = 16
RING = 8
OFFS = (4, 3, -3, 2, -2, 1, -1, 0)
OWN = 7
HALF = RING * ROWS
BF = jnp.bfloat16
F32 = jnp.float32


def slot_of(offset):
    return OFFS.index(4 if offset in (4, -4) else offset)


NEAR = (5, 6, 3, 4)
GI, GT, GXI, GXT, GC = 0, 8, 16, 24, 32
RC, RXI, RXT, RI, RT, RFI, RFT, RDI, RDT = 48, 52, 53, 54, 62, 70, 72, 74, 82
NRECV = 90
NSEND = 100


def kernel(
    img_hbm, txt_hbm, scale_ref, bias_ref, out_i, out_t,
    raw, unit, length, img, txt, grad, own_i, own_t,
    snd_c, snd_xi, snd_xt, snd_ri, snd_rt, snd_li, snd_lt,
    rcv_c, rcv_xi, rcv_xt, rcv_ri, rcv_rt, rcv_fi, rcv_ft, rcv_di, rcv_dt,
    in_sem, ssem, rsem,
):
    loop_at = lax.axis_index("loop")
    grp_at = lax.axis_index("grp")
    c = loop_at % 2
    x = (loop_at // 2) % 4
    y_hi = loop_at // 8
    y_lo = grp_at // 8
    z = grp_at % 8
    y = y_hi * 2 + y_lo

    def device(dx, dy, dz, dc):
        return {"loop": ((dy // 2) * 4 + dx) * 2 + dc, "grp": (dy % 2) * 8 + dz}

    i_peer = {o: device(x, (y + o + RING) % RING, z, c) for o in OFFS[1:-1]}
    t_peer = {o: device(x, y, (z + o + RING) % RING, c) for o in OFFS[1:-1]}
    xa = 3 - x
    xb = x + 1 - 2 * (x % 2)
    xa_peer = device(xa, y, z, c)
    xb_peer = device(xb, y, z, c)
    xi_peer = {o: device(xa, (y + o + RING) % RING, z, c) for o in (1, -1, 2, -2)}
    xt_peer = {o: device(xb, y, (z + o + RING) % RING, c) for o in (1, -1, 2, -2)}
    c_peer = device(x, y, z, 1 - c)

    loads = [
        pltpu.make_async_copy(img_hbm, raw.at[0], in_sem.at[0]),
        pltpu.make_async_copy(txt_hbm, raw.at[1], in_sem.at[1]),
    ]
    for load in loads:
        load.start()

    barrier = pltpu.get_barrier_semaphore()
    peers = []
    for o in (3, -3, 2, -2, 1, -1):
        peers += [table[o] for table in (t_peer, i_peer, xt_peer, xi_peer) if o in table]
    peers += [xb_peer, xa_peer, c_peer]
    for peer in peers:
        pl.semaphore_signal(barrier, 1, device_id=peer, device_id_type=pl.DeviceIdType.MESH)

    def rows(ref, quarter, slot, count=1):
        return ref.at[pl.ds(quarter * HALF + slot * ROWS, count * ROWS)]

    sent = []

    def send(src, dst, r_at, peer):
        copy = pltpu.make_async_remote_copy(
            src, dst, ssem.at[len(sent)], rsem.at[r_at],
            device_id=peer, device_id_type=pl.DeviceIdType.MESH,
        )
        copy.start()
        sent.append(copy)

    def wait_recv(dst, r_at):
        pltpu.make_async_remote_copy(
            dst, dst, ssem.at[0], rsem.at[r_at],
            device_id=c_peer, device_id_type=pl.DeviceIdType.MESH,
        ).wait_recv()

    def normalize(k, table):
        loads[k].wait()
        wide = raw[k].astype(F32)
        norm = jnp.sqrt(jnp.sum(wide * wide, axis=-1, keepdims=True) + EPS)
        units = wide / norm
        unit[k] = units
        length[k] = norm
        table[pl.ds(OWN * ROWS, ROWS)] = units.astype(BF)

    normalize(1, txt)
    pl.semaphore_wait(barrier, len(peers))
    def span(lo, hi):
        return pl.ds(lo * ROWS, (hi - lo) * ROWS)

    def text_part(q, lo, hi):
        part = grad[:, pl.ds(q * HALF + lo * ROWS, (hi - lo) * ROWS)]
        return lax.dot_general(part, img[...], (((0,), (0,)), ((), ())), preferred_element_type=F32)

    def image_part(q, lo, hi):
        part = grad[pl.ds(q * HALF + lo * ROWS, (hi - lo) * ROWS), :]
        return jnp.dot(part, txt[...], preferred_element_type=F32)

    def gather():
        sides = (
            (txt, GT, GXT, t_peer, xt_peer, xb_peer),
            (img, GI, GXI, i_peer, xi_peer, xa_peer),
        )
        for ref, sem, sem_x, ring, diag, pair in sides:
            if ref is img:
                normalize(0, img)
            for s in (1, 2):
                t = slot_of(-OFFS[s])
                send(rows(ref, 0, OWN), rows(ref, 0, t), sem + t, ring[OFFS[s]])
        for ref, sem, sem_x, ring, diag, pair in sides:
            send(rows(ref, 0, OWN), rows(ref, 1, OWN), sem_x + OWN, pair)
        for s in NEAR:
            for ref, sem, sem_x, ring, diag, pair in sides:
                t = slot_of(-OFFS[s])
                send(rows(ref, 0, OWN), rows(ref, 0, t), sem + t, ring[OFFS[s]])
                send(rows(ref, 0, OWN), rows(ref, 1, t), sem_x + t, diag[OFFS[s]])
        for ref, sem, sem_x, ring, diag, pair in sides:
            wait_recv(rows(ref, 0, 1), sem + 1)
            send(rows(ref, 0, 1), rows(ref, 0, 0), sem, ring[-1])
            send(rows(ref, 0, 1), rows(ref, 1, 0), sem_x, diag[-1])
            wait_recv(rows(ref, 0, 2), sem + 2)
            send(rows(ref, 0, 1, 2), rows(ref, 1, 1, 2), sem_x + 1, pair)

        def share(q, lo, n):
            send(rows(txt, q, lo, n), rows(txt, 2 + q, lo, n), GC + q * RING + lo, c_peer)

        share(0, 1, 2)
        for q, sem in ((0, GT), (1, GXT)):
            for s in NEAR:
                wait_recv(rows(txt, q, s), sem + s)
            if q == 1:
                wait_recv(rows(txt, q, OWN), sem + OWN)
            share(q, 3, 5)
        wait_recv(rows(txt, 0, 0), GT)
        share(0, 0, 1)
        wait_recv(rows(txt, 1, 1, 2), GXT + 1)
        share(1, 1, 2)
        wait_recv(rows(txt, 1, 0), GXT)
        share(1, 0, 1)
        for q, sem in ((0, GI), (1, GXI)):
            for s in NEAR:
                wait_recv(rows(img, q, s), sem + s)
            wait_recv(rows(img, q, 0), sem)
        wait_recv(rows(img, 1, OWN), GXI + OWN)
        wait_recv(rows(img, 1, 1, 2), GXI + 1)

    def gather_end():
        for q in (0, 1):
            for lo, n in ((3, 5), (1, 2), (0, 1)):
                wait_recv(rows(txt, 2 + q, lo, n), GC + q * RING + lo)

    def grads():
        scale = jnp.exp(jnp.full((1, 1), scale_ref[0], F32))
        offset = bias_ref[0]
        for q in range(4):
            if q == 2:
                gather_end()
            dots = lax.dot_general(
                img[...], txt[pl.ds(q * HALF, HALF)], (((1,), (1,)), ((), ())), preferred_element_type=F32
            )
            prob = jax.nn.sigmoid(scale * dots + offset)
            if q == 0:
                i = lax.broadcasted_iota(jnp.int32, prob.shape, 0)
                j = lax.broadcasted_iota(jnp.int32, prob.shape, 1)
                prob = prob - jnp.where((i == j) & (i >= OWN * ROWS), 1.0, 0.0)
            grad[:, pl.ds(q * HALF, HALF)] = (scale * prob).astype(BF)

    def reduce():
        def cross_far(snd, rcv_x, rcv_f, sem_x, sem_f, pair, diag):
            send(rows(snd, 0, 1, 2), rcv_x, sem_x, pair)
            send(rows(snd, 0, 0), rows(rcv_f, 0, 1), sem_f + 1, diag[-1])

        def along_far(snd, rcv_f, sem_f, ring):
            send(rows(snd, 0, 0), rows(rcv_f, 0, 0), sem_f, ring[1])

        def near(snd_x, snd, rcv_d, rcv, sem_d, sem, pair, diag, ring):
            for s in NEAR:
                t = slot_of(-OFFS[s])
                send(rows(snd_x, 0, s), rows(rcv_d, 0, t), sem_d + t, diag[OFFS[s]])
                send(rows(snd, 0, s), rows(rcv, 0, t), sem + t, ring[OFFS[s]])
            send(rows(snd_x, 0, OWN), rows(rcv_d, 0, OWN), sem_d + OWN, pair)

        def last(own, snd_l, rcv_x, rcv_f, rcv, sem_x, sem_f, sem, ring):
            wait_recv(rcv_x, sem_x)
            wait_recv(rows(rcv_f, 0, 0), sem_f)
            wait_recv(rows(rcv_f, 0, 1), sem_f + 1)
            snd_l[...] = (own[span(1, 3)] + rcv_x[...].astype(F32) + rcv_f[...].astype(F32)).astype(BF)
            for s in (1, 2):
                t = slot_of(-OFFS[s])
                send(rows(snd_l, 0, s - 1), rows(rcv, 0, t), sem + t, ring[OFFS[s]])

        def core_out(lo, hi, sem):
            for h in (1, 0):
                at = pl.ds(h * HALF + lo * ROWS, (hi - lo) * ROWS)
                snd_c[at] = text_part(2 + h, lo, hi).astype(BF)
                send(snd_c.at[at], rcv_c.at[at], sem + h, c_peer)

        def core_in(h, lo, hi, sem):
            at = pl.ds(h * HALF + lo * ROWS, (hi - lo) * ROWS)
            wait_recv(rcv_c.at[at], sem + h)
            return rcv_c[at].astype(F32)

        far, rest = (0, 3), (3, RING)
        core_out(*far, RC)
        snd_xi[span(*far)] = image_part(1, *far).astype(BF)
        cross_far(snd_xi, rcv_xi, rcv_fi, RXI, RFI, xa_peer, xi_peer)
        own_i[span(*far)] = image_part(0, *far)
        snd_ri[span(0, 1)] = own_i[span(0, 1)].astype(BF)
        along_far(snd_ri, rcv_fi, RFI, i_peer)
        core_out(*rest, RC + 2)
        cross_t = text_part(1, *far)
        along_t = text_part(0, *far)
        snd_xt[span(*far)] = (cross_t + core_in(1, *far, RC)).astype(BF)
        cross_far(snd_xt, rcv_xt, rcv_ft, RXT, RFT, xb_peer, xt_peer)
        own_t[span(*far)] = along_t + core_in(0, *far, RC)
        snd_rt[span(0, 1)] = own_t[span(0, 1)].astype(BF)
        along_far(snd_rt, rcv_ft, RFT, t_peer)
        snd_xi[span(*rest)] = image_part(1, *rest).astype(BF)
        own_i[span(*rest)] = image_part(0, *rest)
        snd_ri[span(*rest)] = own_i[span(*rest)].astype(BF)
        near(snd_xi, snd_ri, rcv_di, rcv_ri, RDI, RI, xa_peer, xi_peer, i_peer)
        snd_xt[span(*rest)] = (text_part(1, *rest) + core_in(1, *rest, RC + 2)).astype(BF)
        own_t[span(*rest)] = text_part(0, *rest) + core_in(0, *rest, RC + 2)
        snd_rt[span(*rest)] = own_t[span(*rest)].astype(BF)
        near(snd_xt, snd_rt, rcv_dt, rcv_rt, RDT, RT, xb_peer, xt_peer, t_peer)
        last(own_i, snd_li, rcv_xi, rcv_fi, rcv_ri, RXI, RFI, RI, i_peer)
        last(own_t, snd_lt, rcv_xt, rcv_ft, rcv_rt, RXT, RFT, RT, t_peer)

    def finish():
        tables = (
            (own_i, rcv_ri, rcv_di, RI, RDI, out_i),
            (own_t, rcv_rt, rcv_dt, RT, RDT, out_t),
        )
        totals = []
        for own, rcv, rcv_d, sem, sem_d, out in tables:
            total = own[pl.ds(OWN * ROWS, ROWS)]
            for s in (OWN, *NEAR):
                wait_recv(rows(rcv_d, 0, s), sem_d + s)
                total = total + rcv_d[pl.ds(s * ROWS, ROWS)].astype(F32)
                if s != OWN:
                    wait_recv(rows(rcv, 0, s), sem + s)
                    total = total + rcv[pl.ds(s * ROWS, ROWS)].astype(F32)
            totals.append(total)
        for k, (own, rcv, rcv_d, sem, sem_d, out) in enumerate(tables):
            total = totals[k]
            for s in (1, 2):
                wait_recv(rows(rcv, 0, s), sem + s)
                total = total + rcv[pl.ds(s * ROWS, ROWS)].astype(F32)
            units = unit[k]
            along = jnp.sum(units * total, axis=-1, keepdims=True)
            out[...] = (total - units * along) / length[k]

    def drain():
        for copy in sent:
            copy.wait_send()
        sent.clear()

    gather()
    grads()
    reduce()
    finish()
    drain()


def per_device(image_emb, text_emb, log_scale, bias):
    rows, width = image_emb.shape
    out = jax.ShapeDtypeStruct((rows, width), F32)
    vmem = lambda n, dtype: pltpu.VMEM((n, width), dtype)
    return pl.pallas_call(
        kernel,
        out_shape=(out, out),
        in_specs=[pl.BlockSpec(memory_space=pl.ANY)] * 2 + [pl.BlockSpec(memory_space=pltpu.SMEM)] * 2,
        out_specs=(pl.BlockSpec(memory_space=pltpu.VMEM),) * 2,
        scratch_shapes=[
            pltpu.VMEM((2, rows, width), BF),
            pltpu.VMEM((2, rows, width), F32),
            pltpu.VMEM((2, rows, 1), F32),
            vmem(2 * HALF, BF),
            vmem(4 * HALF, BF),
            pltpu.VMEM((2 * HALF, 4 * HALF), BF),
            vmem(HALF, F32),
            vmem(HALF, F32),
            vmem(2 * HALF, BF),
            vmem(HALF, BF),
            vmem(HALF, BF),
            vmem(HALF, BF),
            vmem(HALF, BF),
            vmem(2 * ROWS, BF),
            vmem(2 * ROWS, BF),
            vmem(2 * HALF, BF),
            vmem(2 * ROWS, BF),
            vmem(2 * ROWS, BF),
            vmem(HALF, BF),
            vmem(HALF, BF),
            vmem(2 * ROWS, BF),
            vmem(2 * ROWS, BF),
            vmem(HALF, BF),
            vmem(HALF, BF),
            pltpu.SemaphoreType.DMA((2,)),
            pltpu.SemaphoreType.DMA((NSEND,)),
            pltpu.SemaphoreType.DMA((NRECV,)),
        ],
        compiler_params=pltpu.CompilerParams(
            collective_id=0, has_side_effects=True, vmem_limit_bytes=48 * 2**20
        ),
        name="siglip_grads",
    )(
        pltpu.with_memory_space_constraint(image_emb, pltpu.HBM),
        pltpu.with_memory_space_constraint(text_emb, pltpu.HBM),
        log_scale,
        bias,
    )


def solution(mesh):
    return jax.shard_map(
        per_device,
        mesh=mesh,
        in_specs=(P(("loop", "grp"), None), P(("loop", "grp"), None), P(), P()),
        out_specs=(P(("loop", "grp"), None), P(("loop", "grp"), None)),
        check_vma=False,
    )
```

```python
import jax
import jax.numpy as jnp
from jax import lax
from jax.experimental import pallas as pl
from jax.experimental.pallas import tpu as pltpu
from jax.sharding import PartitionSpec as P

EPS = 1e-06
ROWS = 16
RING = 8
OFFS = (4, 3, -3, 2, -2, 1, -1, 0)
OWN = 7
HALF = RING * ROWS
BF = jnp.bfloat16
F32 = jnp.float32


def slot_of(offset):
    return OFFS.index(4 if offset in (4, -4) else offset)


NEAR = (5, 6, 3, 4)
GI, GT, GXI, GXT, GC = 0, 8, 16, 24, 32
RC, RXI, RXT, RI, RT, RFI, RFT, RDI, RDT = 48, 52, 54, 56, 64, 72, 74, 76, 84
NRECV = 92
NSEND = 100


def kernel(
    img_hbm, txt_hbm, scale_ref, bias_ref, sums, unit, length,
    raw, img, txt, grad, own_i, own_t,
    snd_c, snd_xi, snd_xt, snd_ri, snd_rt, snd_li, snd_lt,
    rcv_c, rcv_xi, rcv_xt, rcv_ri, rcv_rt, rcv_fi, rcv_ft, rcv_di, rcv_dt,
    in_sem, ssem, rsem,
):
    loop_at = lax.axis_index("loop")
    grp_at = lax.axis_index("grp")
    c = loop_at % 2
    x = (loop_at // 2) % 4
    y_hi = loop_at // 8
    y_lo = grp_at // 8
    z = grp_at % 8
    y = y_hi * 2 + y_lo

    def device(dx, dy, dz, dc):
        return {"loop": ((dy // 2) * 4 + dx) * 2 + dc, "grp": (dy % 2) * 8 + dz}

    i_peer = {o: device(x, (y + o + RING) % RING, z, c) for o in OFFS[1:-1]}
    t_peer = {o: device(x, y, (z + o + RING) % RING, c) for o in OFFS[1:-1]}
    xa = 3 - x
    xb = x + 1 - 2 * (x % 2)
    xa_peer = device(xa, y, z, c)
    xb_peer = device(xb, y, z, c)
    xi_peer = {o: device(xa, (y + o + RING) % RING, z, c) for o in (1, -1, 2, -2)}
    xt_peer = {o: device(xb, y, (z + o + RING) % RING, c) for o in (1, -1, 2, -2)}
    c_peer = device(x, y, z, 1 - c)

    loads = [
        pltpu.make_async_copy(img_hbm, raw.at[0], in_sem.at[0]),
        pltpu.make_async_copy(txt_hbm, raw.at[1], in_sem.at[1]),
    ]
    for load in loads:
        load.start()

    barrier = pltpu.get_barrier_semaphore()
    peers = []
    for o in (3, -3, 2, -2, 1, -1):
        peers += [table[o] for table in (t_peer, i_peer, xt_peer, xi_peer) if o in table]
    peers += [xb_peer, xa_peer, c_peer]
    for peer in peers:
        pl.semaphore_signal(barrier, 1, device_id=peer, device_id_type=pl.DeviceIdType.MESH)

    def rows(ref, quarter, slot, count=1):
        return ref.at[pl.ds(quarter * HALF + slot * ROWS, count * ROWS)]

    sent = []

    def send(src, dst, r_at, peer):
        copy = pltpu.make_async_remote_copy(
            src, dst, ssem.at[len(sent)], rsem.at[r_at],
            device_id=peer, device_id_type=pl.DeviceIdType.MESH,
        )
        copy.start()
        sent.append(copy)

    def wait_recv(dst, r_at):
        pltpu.make_async_remote_copy(
            dst, dst, ssem.at[0], rsem.at[r_at],
            device_id=c_peer, device_id_type=pl.DeviceIdType.MESH,
        ).wait_recv()

    def normalize(k, table):
        loads[k].wait()
        wide = raw[k].astype(F32)
        norm = jnp.sqrt(jnp.sum(wide * wide, axis=-1, keepdims=True) + EPS)
        units = wide / norm
        unit[k] = units
        length[k] = norm
        table[pl.ds(OWN * ROWS, ROWS)] = units.astype(BF)

    normalize(1, txt)
    pl.semaphore_wait(barrier, len(peers))
    def span(lo, hi):
        return pl.ds(lo * ROWS, (hi - lo) * ROWS)

    def text_part(q, lo, hi):
        part = grad[:, pl.ds(q * HALF + lo * ROWS, (hi - lo) * ROWS)]
        return lax.dot_general(part, img[...], (((0,), (0,)), ((), ())), preferred_element_type=F32)

    def image_part(q, lo, hi):
        part = grad[pl.ds(q * HALF + lo * ROWS, (hi - lo) * ROWS), :]
        return jnp.dot(part, txt[...], preferred_element_type=F32)

    def gather():
        sides = (
            (txt, GT, GXT, t_peer, xt_peer, xb_peer),
            (img, GI, GXI, i_peer, xi_peer, xa_peer),
        )
        for ref, sem, sem_x, ring, diag, pair in sides:
            if ref is img:
                normalize(0, img)
            for s in (1, 2):
                t = slot_of(-OFFS[s])
                send(rows(ref, 0, OWN), rows(ref, 0, t), sem + t, ring[OFFS[s]])
        for ref, sem, sem_x, ring, diag, pair in sides:
            send(rows(ref, 0, OWN), rows(ref, 1, OWN), sem_x + OWN, pair)
        for s in NEAR:
            for ref, sem, sem_x, ring, diag, pair in sides:
                t = slot_of(-OFFS[s])
                send(rows(ref, 0, OWN), rows(ref, 0, t), sem + t, ring[OFFS[s]])
                send(rows(ref, 0, OWN), rows(ref, 1, t), sem_x + t, diag[OFFS[s]])
        for ref, sem, sem_x, ring, diag, pair in sides:
            wait_recv(rows(ref, 0, 1), sem + 1)
            send(rows(ref, 0, 1), rows(ref, 0, 0), sem, ring[-1])
            send(rows(ref, 0, 1), rows(ref, 1, 0), sem_x, diag[-1])
            wait_recv(rows(ref, 0, 2), sem + 2)
            send(rows(ref, 0, 1, 2), rows(ref, 1, 1, 2), sem_x + 1, pair)

        def share(q, lo, n):
            send(rows(txt, q, lo, n), rows(txt, 2 + q, lo, n), GC + q * RING + lo, c_peer)

        share(0, 1, 2)
        for q, sem in ((0, GT), (1, GXT)):
            for s in NEAR:
                wait_recv(rows(txt, q, s), sem + s)
            if q == 1:
                wait_recv(rows(txt, q, OWN), sem + OWN)
            share(q, 3, 5)
        wait_recv(rows(txt, 0, 0), GT)
        share(0, 0, 1)
        wait_recv(rows(txt, 1, 1, 2), GXT + 1)
        share(1, 1, 2)
        wait_recv(rows(txt, 1, 0), GXT)
        share(1, 0, 1)
        for q, sem in ((0, GI), (1, GXI)):
            for s in NEAR:
                wait_recv(rows(img, q, s), sem + s)
            wait_recv(rows(img, q, 0), sem)
        wait_recv(rows(img, 1, OWN), GXI + OWN)
        wait_recv(rows(img, 1, 1, 2), GXI + 1)

    def gather_end():
        for q in (0, 1):
            for lo, n in ((3, 5), (1, 2), (0, 1)):
                wait_recv(rows(txt, 2 + q, lo, n), GC + q * RING + lo)

    def grads():
        scale = jnp.exp(jnp.full((1, 1), scale_ref[0], F32))
        offset = bias_ref[0]
        for q in range(4):
            if q == 2:
                gather_end()
            dots = lax.dot_general(
                img[...], txt[pl.ds(q * HALF, HALF)], (((1,), (1,)), ((), ())), preferred_element_type=F32
            )
            prob = jax.nn.sigmoid(scale * dots + offset)
            if q == 0:
                i = lax.broadcasted_iota(jnp.int32, prob.shape, 0)
                j = lax.broadcasted_iota(jnp.int32, prob.shape, 1)
                prob = prob - jnp.where((i == j) & (i >= OWN * ROWS), 1.0, 0.0)
            grad[:, pl.ds(q * HALF, HALF)] = (scale * prob).astype(BF)

    def reduce():
        def cross_far(snd, rcv_x, rcv_f, sem_x, sem_f, pair, diag):
            send(rows(snd, 0, 0), rows(rcv_f, 0, 1), sem_f + 1, diag[-1])
            for s in (1, 2):
                send(rows(snd, 0, s), rows(rcv_x, 0, s - 1), sem_x + s - 1, pair)

        def along_far(snd, rcv_f, sem_f, ring):
            send(rows(snd, 0, 0), rows(rcv_f, 0, 0), sem_f, ring[1])

        def near(snd_x, snd, rcv_d, rcv, sem_d, sem, pair, diag, ring):
            for s in (3, 4, 5, 6):
                t = slot_of(-OFFS[s])
                send(rows(snd_x, 0, s), rows(rcv_d, 0, t), sem_d + t, diag[OFFS[s]])
                send(rows(snd, 0, s), rows(rcv, 0, t), sem + t, ring[OFFS[s]])
            send(rows(snd_x, 0, OWN), rows(rcv_d, 0, OWN), sem_d + OWN, pair)

        def last(own, snd_l, rcv_x, rcv_f, rcv, sem_x, sem_f, sem, ring):
            for s in (1, 2):
                at = span(s - 1, s)
                wait_recv(rows(rcv_f, 0, s - 1), sem_f + s - 1)
                wait_recv(rcv_x.at[at], sem_x + s - 1)
                snd_l[at] = (own[span(s, s + 1)] + rcv_x[at].astype(F32) + rcv_f[at].astype(F32)).astype(BF)
                t = slot_of(-OFFS[s])
                send(rows(snd_l, 0, s - 1), rows(rcv, 0, t), sem + t, ring[OFFS[s]])

        def core_out(lo, hi, sem):
            for h in (1, 0):
                at = pl.ds(h * HALF + lo * ROWS, (hi - lo) * ROWS)
                snd_c[at] = text_part(2 + h, lo, hi).astype(BF)
                send(snd_c.at[at], rcv_c.at[at], sem + h, c_peer)

        def core_in(h, lo, hi, sem):
            at = pl.ds(h * HALF + lo * ROWS, (hi - lo) * ROWS)
            wait_recv(rcv_c.at[at], sem + h)
            return rcv_c[at].astype(F32)

        far, rest = (0, 3), (3, RING)
        core_out(*far, RC)
        snd_xi[span(*far)] = image_part(1, *far).astype(BF)
        cross_far(snd_xi, rcv_xi, rcv_fi, RXI, RFI, xa_peer, xi_peer)
        own_i[span(*far)] = image_part(0, *far)
        snd_ri[span(0, 1)] = own_i[span(0, 1)].astype(BF)
        along_far(snd_ri, rcv_fi, RFI, i_peer)
        core_out(*rest, RC + 2)
        cross_t = text_part(1, *far)
        along_t = text_part(0, *far)
        snd_xt[span(*far)] = (cross_t + core_in(1, *far, RC)).astype(BF)
        cross_far(snd_xt, rcv_xt, rcv_ft, RXT, RFT, xb_peer, xt_peer)
        own_t[span(*far)] = along_t + core_in(0, *far, RC)
        snd_rt[span(0, 1)] = own_t[span(0, 1)].astype(BF)
        along_far(snd_rt, rcv_ft, RFT, t_peer)
        snd_xi[span(*rest)] = image_part(1, *rest).astype(BF)
        own_i[span(*rest)] = image_part(0, *rest)
        snd_ri[span(*rest)] = own_i[span(*rest)].astype(BF)
        near(snd_xi, snd_ri, rcv_di, rcv_ri, RDI, RI, xa_peer, xi_peer, i_peer)
        snd_xt[span(*rest)] = (text_part(1, *rest) + core_in(1, *rest, RC + 2)).astype(BF)
        own_t[span(*rest)] = text_part(0, *rest) + core_in(0, *rest, RC + 2)
        snd_rt[span(*rest)] = own_t[span(*rest)].astype(BF)
        near(snd_xt, snd_rt, rcv_dt, rcv_rt, RDT, RT, xb_peer, xt_peer, t_peer)
        last(own_i, snd_li, rcv_xi, rcv_fi, rcv_ri, RXI, RFI, RI, i_peer)
        last(own_t, snd_lt, rcv_xt, rcv_ft, rcv_rt, RXT, RFT, RT, t_peer)

    def finish():
        tables = (
            (own_i, rcv_ri, rcv_di, RI, RDI),
            (own_t, rcv_rt, rcv_dt, RT, RDT),
        )
        totals = []
        for own, rcv, rcv_d, sem, sem_d in tables:
            total = own[pl.ds(OWN * ROWS, ROWS)]
            for s in (OWN, *NEAR):
                wait_recv(rows(rcv_d, 0, s), sem_d + s)
                total = total + rcv_d[pl.ds(s * ROWS, ROWS)].astype(F32)
                if s != OWN:
                    wait_recv(rows(rcv, 0, s), sem + s)
                    total = total + rcv[pl.ds(s * ROWS, ROWS)].astype(F32)
            totals.append(total)
        for k, (own, rcv, rcv_d, sem, sem_d) in enumerate(tables):
            total = totals[k]
            for s in (1, 2):
                wait_recv(rows(rcv, 0, s), sem + s)
                total = total + rcv[pl.ds(s * ROWS, ROWS)].astype(F32)
            sums[k] = total

    def drain():
        for copy in sent:
            copy.wait_send()
        sent.clear()

    gather()
    grads()
    reduce()
    finish()
    drain()


def project(sums, unit, length, out_i, out_t, rows, sem):
    copies = []
    for k, out in enumerate((out_i, out_t)):
        units = unit[k]
        total = sums[k]
        along = jnp.sum(units * total, axis=-1, keepdims=True)
        rows[k] = (total - units * along) / length[k]
        copies.append(pltpu.make_async_copy(rows.at[k], out, sem.at[k]))
        copies[k].start()
    for copy in copies:
        copy.wait()


def per_device(image_emb, text_emb, log_scale, bias):
    rows, width = image_emb.shape
    out = jax.ShapeDtypeStruct((rows, width), F32)
    vmem = lambda n, dtype: pltpu.VMEM((n, width), dtype)
    wide = jax.ShapeDtypeStruct((2, rows, width), F32)
    parts = pl.pallas_call(
        kernel,
        out_shape=(wide, wide, jax.ShapeDtypeStruct((2, rows, 1), F32)),
        in_specs=[pl.BlockSpec(memory_space=pl.ANY)] * 2 + [pl.BlockSpec(memory_space=pltpu.SMEM)] * 2,
        out_specs=(pl.BlockSpec(memory_space=pltpu.VMEM),) * 3,
        scratch_shapes=[
            pltpu.VMEM((2, rows, width), BF),
            vmem(2 * HALF, BF),
            vmem(4 * HALF, BF),
            pltpu.VMEM((2 * HALF, 4 * HALF), BF),
            vmem(HALF, F32),
            vmem(HALF, F32),
            vmem(2 * HALF, BF),
            vmem(HALF, BF),
            vmem(HALF, BF),
            vmem(HALF, BF),
            vmem(HALF, BF),
            vmem(2 * ROWS, BF),
            vmem(2 * ROWS, BF),
            vmem(2 * HALF, BF),
            vmem(2 * ROWS, BF),
            vmem(2 * ROWS, BF),
            vmem(HALF, BF),
            vmem(HALF, BF),
            vmem(2 * ROWS, BF),
            vmem(2 * ROWS, BF),
            vmem(HALF, BF),
            vmem(HALF, BF),
            pltpu.SemaphoreType.DMA((2,)),
            pltpu.SemaphoreType.DMA((NSEND,)),
            pltpu.SemaphoreType.DMA((NRECV,)),
        ],
        compiler_params=pltpu.CompilerParams(
            collective_id=0, has_side_effects=True, vmem_limit_bytes=48 * 2**20
        ),
        name="siglip_grads",
    )(
        pltpu.with_memory_space_constraint(image_emb, pltpu.HBM),
        pltpu.with_memory_space_constraint(text_emb, pltpu.HBM),
        log_scale,
        bias,
    )
    return pl.pallas_call(
        project,
        out_shape=(out, out),
        in_specs=[pl.BlockSpec(memory_space=pltpu.VMEM)] * 3,
        out_specs=(pl.BlockSpec(memory_space=pltpu.HBM),) * 2,
        scratch_shapes=[pltpu.VMEM((2, rows, width), F32), pltpu.SemaphoreType.DMA((2,))],
        name="project",
    )(*[pltpu.with_memory_space_constraint(part, pltpu.VMEM) for part in parts])


def solution(mesh):
    return jax.shard_map(
        per_device,
        mesh=mesh,
        in_specs=(P(("loop", "grp"), None), P(("loop", "grp"), None), P(), P()),
        out_specs=(P(("loop", "grp"), None), P(("loop", "grp"), None)),
        check_vma=False,
    )
```
